32 devices in a mesh: loop: 8 (over y, x, core), stack: 4 (over z).
Axes of the slice: x: 2, y: 2, z: 4, core: 2. Of those that a mesh axis runs over, the one named last changes fastest.
Arguments:
- spectra: bfloat16 [512, 2, 32, 1024], P('stack', None, None, 'loop'), may hold values from -6 to 6
- channel_loc: int32 [1024], P('loop'), may hold values from 0 to 2047, as said below
- channel_valid: int32 [1024], P('loop'), may hold values 0 or 1
- bin_owner: int32 [32], replicated, may hold values from 0 to 3, as said below
Outputs:
- linear_stack: float32 [4, 16, 1024], P('stack', 'loop')
- phase_stack: float32 [4, 16, 1024], P('stack', 'loop')
The draws below stay inside these ranges and needn't reach their ends.
Inputs may be any that keep to these rules, and one draw needn't show every extreme that they name: `channel_loc`: strictly increasing along the channels; channel c lies at 2 c or 2 c + 1, the first at 0 and the last at 2047. `bin_owner`: at most 16 bins share an owner; some owner holds exactly 16.
All inputs are finite; a program needn't handle non-finite values. No bound on the sum of `channel_valid` on one device may be relied on, other than what follows from the above.
Results may differ from the reference program's by a relative error of at most 0.003.
Values may be sent and summed in bfloat16 or wider, within the bound.
A program may use at most 128 MiB of HBM per device.

```python
import math
import jax
import jax.numpy as jnp
from jax import lax

NFREQ = 512
SEG = 32
BIN_DEV = 8
NCH = 1024
NBIN = 32
BCAP = 16


def draw_channel_loc(key, part):
    positions = jnp.arange(NCH, dtype=jnp.int32)
    jitter = jax.random.randint(key, (NCH,), 0, 2, dtype=jnp.int32)
    jitter = jnp.where(positions == 0, 0, jnp.where(positions == NCH - 1, 1, jitter))
    return (2 * positions + jitter).astype(jnp.int32)


def draw_bin_owner(key, part):
    owner_count = NBIN // BIN_DEV
    key_full = jax.random.fold_in(key, 11)
    key_order = jax.random.fold_in(key, 12)
    key_slots = jax.random.fold_in(key, 13)
    full_owner = jax.random.randint(key_full, (), 0, owner_count, dtype=jnp.int32)
    bin_order = jax.random.permutation(key_order, NBIN).astype(jnp.int32)
    other_slots = jax.random.permutation(key_slots, (owner_count - 1) * BCAP).astype(jnp.int32)
    others = other_slots[:NBIN - BCAP] // BCAP
    others = others + (others >= full_owner).astype(jnp.int32)
    in_order = jnp.concatenate([jnp.full((BCAP,), full_owner, jnp.int32), others])
    return jnp.zeros((NBIN,), jnp.int32).at[bin_order].set(in_order)


def place_ends(drawn, rng, low, top_value):
    dims = drawn.shape
    index_at = [jax.random.randint(jax.random.fold_in(rng, axis), (), 0, dims[axis]) for axis in range(len(dims))]
    drawn = drawn.at[tuple(index_at)].set(low)
    longest = dims.index(max(dims))
    index_at[longest] = (index_at[longest] + 1) % dims[longest]
    return drawn.at[tuple(index_at)].set(top_value)


def shard_levels(stream_key, extent, shards, low, high):
    def one(dim, blocks):
        draws = jax.random.uniform(jax.random.fold_in(jax.random.fold_in(stream_key, 6), dim), (blocks,), jnp.float32, low / len(shards), high / len(shards))
        return jnp.repeat(jnp.exp(draws), extent[dim] // blocks).reshape((-1,) + (1,) * (len(extent) - dim - 1))

    level = one(*shards[0])
    for cut in shards[1:]:
        level = level * one(*cut)
    return level


def bell_draw(key, extent, width, most, cuts=(), kind=jnp.bfloat16):
    level = shard_levels(key, extent, cuts, -0.22, 0.18) if cuts else 1.0
    array = jax.random.normal(key, extent, jnp.float32) * width * level
    return jnp.minimum(jnp.maximum(array, -most), most).astype(kind)


def setup_inputs(seed: int = 0) -> dict:
    seeds = jax.random.split(jax.random.key(seed), 5)
    return {
        "spectra": bell_draw(seeds[0], (NFREQ, 2, SEG, NCH), 1.0, 6.0, ((0, 4), (3, 8))),
        "channel_loc": draw_channel_loc(jax.random.fold_in(seeds[4], 71), 0),
        "channel_valid": place_ends((jax.random.randint(seeds[2], (NCH,), 0, 8) < 7).astype(jnp.int32), jax.random.fold_in(seeds[2], 1), 0, 1),
        "bin_owner": draw_bin_owner(jax.random.fold_in(seeds[4], 71), 0),
    }


def lag_matrix(freq_count):
    freq_ids = jnp.arange(freq_count, dtype=jnp.int32)
    lag_ids = jnp.arange(2 * freq_count, dtype=jnp.int32) - freq_count
    turn_count = freq_ids[:, None] * lag_ids[None, :] % (2 * freq_count)
    phase_angle = turn_count.astype(jnp.float32) * (math.pi / freq_count)
    bin_weight = jnp.where(freq_ids == 0, 1.0, 2.0).astype(jnp.float32)[:, None]
    return jnp.concatenate([bin_weight * jnp.cos(phase_angle), -bin_weight * jnp.sin(phase_angle)], 0)

def normalize(series):
    return series / jnp.sqrt(lax.optimization_barrier(jnp.mean(series * series, axis=-1, keepdims=True)) + 1e-06)

def finish(linear_re, linear_im, phase_re, phase_im):
    coherence = phase_re * phase_re + phase_im * phase_im
    matrix = lag_matrix(linear_re.shape[1])
    linear = jnp.dot(jnp.concatenate([linear_re, linear_im], 1), matrix, precision=lax.Precision.HIGHEST)
    weighted = jnp.dot(jnp.concatenate([linear_re * coherence, linear_im * coherence], 1), matrix, precision=lax.Precision.HIGHEST)
    return (normalize(linear), normalize(weighted))

def reference(spectra, channel_loc, channel_valid, bin_owner):
    freq_count = spectra.shape[0]
    chan_count = spectra.shape[3]
    bin_count = bin_owner.shape[0]
    bin_width = 2 * chan_count // bin_count
    values_f = spectra.astype(jnp.float32)
    left_side = jnp.stack([values_f, jnp.stack([values_f[:, 1], -values_f[:, 0]], 1)], 1)
    valid_f = channel_valid.astype(jnp.float32)
    labels = jnp.arange(bin_count, dtype=jnp.int32)
    row_count = 16

    def add_block(running, block_index):
        first_row = (block_index * row_count).astype(jnp.int32)
        row_block = lax.dynamic_slice_in_dim(left_side, first_row, row_count, 4)
        products = jnp.einsum('fkpsa,fpsb->fkab', row_block, values_f, precision=lax.Precision.HIGHEST)
        real_part = products[:, 0]
        imag_part = products[:, 1]
        magnitude = jnp.maximum(jnp.sqrt(real_part * real_part + imag_part * imag_part), 1.0)
        components = jnp.stack([real_part, imag_part, real_part / magnitude, imag_part / magnitude], 1).astype(jnp.bfloat16)
        components = lax.optimization_barrier(components).astype(jnp.float32).reshape(freq_count * 4, row_count * chan_count)
        row_loc = lax.dynamic_slice_in_dim(channel_loc, first_row, row_count)
        row_valid = lax.dynamic_slice_in_dim(valid_f, first_row, row_count)
        loc_gap = channel_loc[None, :] - row_loc[:, None]
        weight = jnp.where(loc_gap > 0, row_valid[:, None] * valid_f[None, :], 0.0)
        pair_bin = jnp.where(loc_gap > 0, loc_gap // bin_width, 0)
        onehot = jnp.where(pair_bin[:, :, None] == labels, weight[:, :, None], 0.0).reshape(row_count * chan_count, bin_count)
        return (running + jnp.dot(components, onehot, precision=lax.Precision.HIGHEST), None)
    start_sum = jnp.zeros((freq_count * 4, bin_count), jnp.float32)
    running, _ = lax.scan(add_block, start_sum, jnp.arange(chan_count // row_count, dtype=jnp.int32))
    bin_sums = running.reshape(freq_count, 4, bin_count)
    linear, weighted = finish(bin_sums[:, 0].T, bin_sums[:, 1].T, bin_sums[:, 2].T, bin_sums[:, 3].T)
    same_owner = bin_owner[:, None] == bin_owner[None, :]
    earlier = labels[None, :] < labels[:, None]
    slot_rank = lax.optimization_barrier(jnp.sum((same_owner & earlier).astype(jnp.int32), axis=1))
    owner_count = bin_count // BIN_DEV
    blank = jnp.zeros((owner_count, BCAP, 2 * freq_count), jnp.float32)
    return (blank.at[bin_owner, slot_rank].set(linear), blank.at[bin_owner, slot_rank].set(weighted))
```

```python
import functools
import math

import jax
import jax.numpy as jnp
import numpy as np
from jax import lax
from jax.experimental import pallas as pl
from jax.experimental.pallas import tpu as pltpu
from jax.sharding import PartitionSpec as P

BCAP = 16
LANES = 128


def lag_matrix(freq_count):
    freq_ids = np.arange(freq_count)
    lag_ids = np.arange(2 * freq_count) - freq_count
    turns = freq_ids[:, None] * lag_ids[None, :] % (2 * freq_count)
    angle = turns * (math.pi / freq_count)
    bin_weight = np.where(freq_ids == 0, 1.0, 2.0)[:, None]
    return np.concatenate(
        [bin_weight * np.cos(angle), -bin_weight * np.sin(angle)], 0
    ).astype(np.float32)


def normalize(series):
    return series / jnp.sqrt(jnp.mean(series * series, axis=-1, keepdims=True) + 1e-06)


def finish(linear_re, linear_im, phase_re, phase_im):
    coherence = phase_re * phase_re + phase_im * phase_im
    matrix = jnp.asarray(lag_matrix(linear_re.shape[1]))
    rows = linear_re.shape[0]
    both = jnp.dot(
        jnp.concatenate(
            [
                jnp.concatenate([linear_re, linear_im], 1),
                jnp.concatenate([linear_re * coherence, linear_im * coherence], 1),
            ],
            0,
        ),
        matrix,
        precision=lax.Precision.HIGHEST,
    )
    both = normalize(both)
    return both[:rows], both[rows:]


def pair_kernel(bin_count, seg2, x_ref, perm_ref, keep_ref, shift_ref, out_ref, left, right):
    groups, freqs = x_ref.shape[0], x_ref.shape[1]
    half = seg2 // 2
    reps = LANES // bin_count

    def fold(block):
        total = block[:bin_count]
        for rep in range(1, reps):
            total = total + block[rep * bin_count : (rep + 1) * bin_count]
        return total

    right[...] = jnp.zeros_like(right)

    def freq_pair(pair, carry):
        rows = jnp.concatenate(
            [x_ref[g, pl.ds(2 * pair, 2)].reshape(2 * seg2, LANES) for g in range(groups)], 1
        )
        for block in range(groups):
            cols = jnp.dot(
                rows,
                perm_ref[:, block * LANES : (block + 1) * LANES],
                preferred_element_type=jnp.float32,
            )
            left[block * LANES : (block + 1) * LANES] = cols.T.astype(jnp.bfloat16)
            for which in range(2):
                at = which * seg2
                re, im = cols[at : at + half], cols[at + half : at + seg2]
                right[block, which, at : at + seg2, :LANES] = cols[at : at + seg2].astype(
                    jnp.bfloat16
                )
                right[block, which, at : at + seg2, LANES:] = jnp.concatenate(
                    [-im, re], 0
                ).astype(jnp.bfloat16)

        def one_freq(which, carry):
            def products(row_block, weights):
                lhs = left[pl.ds(pl.multiple_of(row_block * LANES, LANES), LANES)]
                both = jnp.dot(lhs, weights, preferred_element_type=jnp.float32)
                re, im = both[:, :LANES], both[:, LANES:]
                scale = lax.rsqrt(jnp.maximum(re * re + im * im, 1.0))
                return re, im, re * scale, im * scale

            zero = jnp.zeros((bin_count, LANES), jnp.float32)
            sums, moved = (zero,) * 4, (zero,) * 4
            for block in range(groups):
                weights = right[block, which]

                def add(row_block, sums):
                    parts = products(row_block, weights)
                    return tuple(s + fold(p) for s, p in zip(sums, parts))

                if groups <= 8:
                    for row_block in range(block):
                        sums = add(row_block, sums)
                else:
                    sums = lax.fori_loop(0, block, add, sums)
                parts = products(block, weights)
                keep, shift = keep_ref[block], shift_ref[block]
                sums = tuple(s + fold(p * keep) for s, p in zip(sums, parts))
                moved = tuple(s + fold(p * shift) for s, p in zip(moved, parts))
            for c in range(4):
                out_ref[2 * pair + which, c, 0] = sums[c]
                out_ref[2 * pair + which, c, 1] = moved[c]
            return carry

        return lax.fori_loop(0, 2, one_freq, carry)

    lax.fori_loop(0, freqs // 2, freq_pair, 0)


def on_device(spectra, channel_loc, channel_valid, bin_owner):
    loop_size = lax.axis_size("loop")
    stack_size = lax.axis_size("stack")
    freq_dev, _, seg, channels = spectra.shape
    bin_count = bin_owner.shape[0]
    groups = loop_size
    nch = groups * channels
    hop = nch // bin_count
    freqs = freq_dev // loop_size
    seg2 = 2 * seg
    reps = LANES // bin_count

    x = lax.all_to_all(
        spectra.reshape(loop_size, freqs, seg2, channels), "loop", 0, 0, tiled=True
    )
    table = lax.all_gather(jnp.stack([channel_loc, channel_valid]), "loop", axis=1, tiled=True)
    late = table[0] - 2 * jnp.arange(nch, dtype=jnp.int32)
    valid = table[1]

    chan = jnp.arange(nch, dtype=jnp.int32)
    place = (chan % hop) * bin_count + chan // hop
    perm = jnp.where(
        (place[:, None] == chan[None, :]) & (valid[:, None] > 0), 1.0, 0.0
    ).astype(jnp.bfloat16)
    late = late.reshape(bin_count, hop).T.reshape(groups, LANES)
    lane = jnp.arange(LANES, dtype=jnp.int32)
    rep, step = lane // bin_count, lane % bin_count
    same = (rep[:, None] == rep[None, :]) & (step[None, :] > step[:, None])
    early = late[:, None, :] < late[:, :, None]
    keep = ((rep[:, None] < rep[None, :])[None] | (same[None] & ~early)).astype(jnp.float32)
    shift = (same[None] & early).astype(jnp.float32)

    whole = pl.BlockSpec(memory_space=pltpu.VMEM)
    pair_sums = pl.pallas_call(
        functools.partial(pair_kernel, bin_count, seg2),
        out_shape=jax.ShapeDtypeStruct((freqs, 4, 2, bin_count, LANES), jnp.float32),
        in_specs=[whole] * 4,
        out_specs=whole,
        scratch_shapes=[
            pltpu.VMEM((nch, 2 * seg2), jnp.bfloat16),
            pltpu.VMEM((groups, 2, 2 * seg2, 2 * LANES), jnp.bfloat16),
        ],
        compiler_params=pltpu.CompilerParams(vmem_limit_bytes=48 * 2**20),
        cost_estimate=pl.CostEstimate(
            flops=freqs * nch * nch * seg2 * 2, bytes_accessed=8 * 2**20, transcendentals=0
        ),
    )(x, perm, keep, shift)

    gap = step[None, :] - jnp.arange(bin_count, dtype=jnp.int32)[:, None]
    labels = jnp.arange(bin_count, dtype=jnp.int32)
    ahead = gap[..., None] == labels
    behind = -gap[..., None] - 1 == labels
    below = (gap[..., None] - 1 == labels) & (gap[..., None] > 0)
    to_bin = jnp.stack(
        [jnp.stack([ahead, behind], 2), jnp.stack([below, jnp.zeros_like(below)], 2)], 0
    ).astype(jnp.float32)
    binned = jnp.dot(
        pair_sums.reshape(freqs * 4, 2 * bin_count * LANES),
        to_bin.reshape(2 * bin_count * LANES, 2 * bin_count),
        precision=lax.Precision.HIGHEST,
    ).reshape(freqs, 4, 2, bin_count)
    sign = jnp.array([1.0, -1.0, 1.0, -1.0], jnp.float32)[None, :, None]
    bins = binned[:, :, 0] + sign * binned[:, :, 1]

    same_owner = bin_owner[:, None] == bin_owner[None, :]
    earlier = labels[None, :] < labels[:, None]
    slot_rank = jnp.sum((same_owner & earlier).astype(jnp.int32), axis=1)
    slot = bin_owner * BCAP + slot_rank
    placement = (
        slot[:, None] == jnp.arange(BCAP * stack_size, dtype=jnp.int32)[None, :]
    ).astype(jnp.float32)
    packed = jnp.einsum("bs,fcb->scf", placement, bins, precision=lax.Precision.HIGHEST)
    devices = stack_size * loop_size
    packed = packed.reshape(devices, BCAP // loop_size, 4, freqs)
    owned = lax.all_to_all(packed, ("stack", "loop"), 0, 0, tiled=True)
    row_total = BCAP // loop_size
    sums = owned.transpose(1, 2, 0, 3).reshape(row_total, 4, devices * freqs)
    linear, weighted = finish(sums[:, 0], sums[:, 1], sums[:, 2], sums[:, 3])
    return (linear.reshape(1, row_total, -1), weighted.reshape(1, row_total, -1))


def solution(mesh):
    in_specs = (P("stack", None, None, "loop"), P("loop"), P("loop"), P())
    out_specs = (P("stack", "loop", None), P("stack", "loop", None))
    return jax.shard_map(
        on_device, mesh=mesh, in_specs=in_specs, out_specs=out_specs, check_vma=False
    )
```

```python
import functools
import math

import jax
import jax.numpy as jnp
import numpy as np
from jax import lax
from jax.experimental import pallas as pl
from jax.experimental.pallas import tpu as pltpu
from jax.sharding import PartitionSpec as P

BCAP = 16
LANES = 128


def lag_matrix(freq_count):
    freq_ids = np.arange(freq_count)
    lag_ids = np.arange(2 * freq_count) - freq_count
    turns = freq_ids[:, None] * lag_ids[None, :] % (2 * freq_count)
    angle = turns * (math.pi / freq_count)
    bin_weight = np.where(freq_ids == 0, 1.0, 2.0)[:, None]
    return np.concatenate(
        [bin_weight * np.cos(angle), -bin_weight * np.sin(angle)], 0
    ).astype(np.float32)


def normalize(series):
    return series / jnp.sqrt(jnp.mean(series * series, axis=-1, keepdims=True) + 1e-06)


def finish(linear_re, linear_im, phase_re, phase_im):
    coherence = phase_re * phase_re + phase_im * phase_im
    matrix = jnp.asarray(lag_matrix(linear_re.shape[1]))
    rows = linear_re.shape[0]
    both = jnp.dot(
        jnp.concatenate(
            [
                jnp.concatenate([linear_re, linear_im], 1),
                jnp.concatenate([linear_re * coherence, linear_im * coherence], 1),
            ],
            0,
        ),
        matrix,
        precision=lax.Precision.HIGHEST,
    )
    both = normalize(both)
    return both[:rows], both[rows:]


def pair_kernel(
    bin_count,
    seg2,
    spectra_ref,
    table_ref,
    perm_hbm,
    base_ref,
    out_ref,
    x_ref,
    tables,
    perm_ref,
    keep_ref,
    shift_ref,
    left,
    right,
    send_sem,
    recv_sem,
    table_send,
    table_recv,
    local_sem,
):
    groups, freqs = x_ref.shape[0], x_ref.shape[1]
    half = seg2 // 2
    reps = LANES // bin_count
    me = lax.axis_index("loop")

    def peer(k):
        return lax.rem(me + k, groups)

    own = pltpu.make_async_copy(spectra_ref.at[me], x_ref.at[me], local_sem.at[0])
    own.start()
    fetch = pltpu.make_async_copy(perm_hbm, perm_ref, local_sem.at[1])
    fetch.start()
    own_table = pltpu.make_async_copy(table_ref, tables.at[me], local_sem.at[2])
    own_table.start()

    barrier = pltpu.get_barrier_semaphore()
    for k in range(1, groups):
        pl.semaphore_signal(
            barrier, inc=1, device_id={"loop": peer(k)}, device_id_type=pl.DeviceIdType.MESH
        )
    pl.semaphore_wait(barrier, groups - 1)

    def table_copy(k):
        return pltpu.make_async_remote_copy(
            src_ref=table_ref,
            dst_ref=tables.at[me],
            send_sem=table_send.at[k - 1],
            recv_sem=table_recv.at[k - 1],
            device_id={"loop": peer(k)},
            device_id_type=pl.DeviceIdType.MESH,
        )

    def pair_copy(pair, k):
        return pltpu.make_async_remote_copy(
            src_ref=spectra_ref.at[peer(k), pl.ds(2 * pair, 2)],
            dst_ref=x_ref.at[me, pl.ds(2 * pair, 2)],
            send_sem=send_sem.at[pair, k - 1],
            recv_sem=recv_sem.at[pair, k - 1],
            device_id={"loop": peer(k)},
            device_id_type=pl.DeviceIdType.MESH,
        )

    for k in range(1, groups):
        table_copy(k).start()

    def send_pair(pair, carry):
        for k in range(1, groups):
            pair_copy(pair, k).start()
        return carry

    lax.fori_loop(0, freqs // 2, send_pair, 0)

    def fold(block):
        total = block[:bin_count]
        for rep in range(1, reps):
            total = total + block[rep * bin_count : (rep + 1) * bin_count]
        return total

    right[...] = jnp.zeros_like(right)
    fetch.wait()
    own_table.wait()
    for k in range(1, groups):
        table_copy(k).wait()
    flags = jnp.concatenate([tables[g] for g in range(groups)], 1).astype(jnp.float32)
    valid = flags[1:2].astype(jnp.bfloat16)
    flags = flags.astype(jnp.bfloat16)
    for block in range(groups):
        late = jnp.dot(
            flags,
            perm_ref[:, block * LANES : (block + 1) * LANES],
            preferred_element_type=jnp.float32,
        )[0:1]
        late = jnp.broadcast_to(late, (LANES, LANES))
        early = late.T * (1.0 - late)
        keep_ref[block] = base_ref[0] + base_ref[1] * (1.0 - early)
        shift_ref[block] = base_ref[1] * early
    own.wait()

    row_ids = lax.broadcasted_iota(jnp.int32, (bin_count, LANES), 0)
    lane_ids = lax.broadcasted_iota(jnp.int32, (bin_count, LANES), 1)
    ahead = row_ids <= (lane_ids & (bin_count - 1))

    sub_ids = row_ids[:8]

    def turn(part):
        count = bin_count
        while count > 8:
            count //= 2
            part = part[:count] + pltpu.roll(part[count:], LANES - count, 1)
        for step in (4, 2, 1):
            part = jnp.where((sub_ids & step) != 0, pltpu.roll(part, LANES - step, 1), part)
        return part

    def freq_pair(pair, carry):
        for k in range(1, groups):
            pair_copy(pair, k).wait_recv()
        rows = jnp.concatenate(
            [x_ref[g, pl.ds(2 * pair, 2)].reshape(2 * seg2, LANES) for g in range(groups)], 1
        )
        rows = rows * valid
        for block in range(groups):
            cols = jnp.dot(
                rows,
                perm_ref[:, block * LANES : (block + 1) * LANES],
                preferred_element_type=jnp.float32,
            )
            left[block * LANES : (block + 1) * LANES] = cols.T.astype(jnp.bfloat16)
            for which in range(2):
                at = which * seg2
                re, im = cols[at : at + half], cols[at + half : at + seg2]
                right[block, which, at : at + seg2, :LANES] = cols[at : at + seg2].astype(
                    jnp.bfloat16
                )
                right[block, which, at : at + seg2, LANES:] = jnp.concatenate(
                    [-im, re], 0
                ).astype(jnp.bfloat16)

        def one_freq(which, carry):
            def products(row_block, weights):
                lhs = left[pl.ds(pl.multiple_of(row_block * LANES, LANES), LANES)]
                both = jnp.dot(lhs, weights, preferred_element_type=jnp.float32)
                re, im = both[:, :LANES], both[:, LANES:]
                scale = lax.rsqrt(jnp.maximum(re * re + im * im, 1.0))
                return re, im, re * scale, im * scale

            zero = jnp.zeros((bin_count, LANES), jnp.float32)
            sums, moved = (zero,) * 4, (zero,) * 4
            for block in range(groups):
                weights = right[block, which]

                def add(row_block, sums):
                    parts = products(row_block, weights)
                    return tuple(s + fold(p) for s, p in zip(sums, parts))

                if groups <= 8:
                    for row_block in range(block):
                        sums = add(row_block, sums)
                else:
                    sums = lax.fori_loop(0, block, add, sums)
                parts = products(block, weights)
                keep, shift = keep_ref[block], shift_ref[block]
                sums = tuple(s + fold(p * keep) for s, p in zip(sums, parts))
                moved = tuple(s + fold(p * shift) for s, p in zip(moved, parts))
            for c in range(4):
                both = (
                    jnp.where(ahead, sums[c], 0.0),
                    jnp.where(ahead, 0.0, sums[c]),
                    moved[c],
                )
                for n, part in enumerate(both):
                    out_ref[2 * pair + which, 3 * c + n] = jnp.sum(turn(part), axis=0)
            return carry

        return lax.fori_loop(0, 2, one_freq, carry)

    lax.fori_loop(0, freqs // 2, freq_pair, 0)

    def sent(pair, carry):
        for k in range(1, groups):
            pair_copy(pair, k).wait_send()
        return carry

    lax.fori_loop(0, freqs // 2, sent, 0)


def on_device(spectra, channel_loc, channel_valid, bin_owner):
    loop_size = lax.axis_size("loop")
    stack_size = lax.axis_size("stack")
    freq_dev, _, seg, channels = spectra.shape
    bin_count = bin_owner.shape[0]
    groups = loop_size
    nch = groups * channels
    hop = nch // bin_count
    freqs = freq_dev // loop_size
    seg2 = 2 * seg
    reps = LANES // bin_count

    x = spectra.reshape(loop_size, freqs, seg2, channels)
    first = lax.axis_index("loop") * channels
    late = channel_loc - 2 * (first + jnp.arange(channels, dtype=jnp.int32))
    table = jnp.pad(jnp.stack([late, channel_valid]), ((0, 6), (0, 0)))

    chan = np.arange(nch)
    place = (chan % hop) * bin_count + chan // hop
    perm = jnp.asarray(place[:, None] == chan[None, :], jnp.bfloat16)
    lane = np.arange(LANES)
    rep, step = lane // bin_count, lane % bin_count
    same = (rep[:, None] == rep[None, :]) & (step[None, :] > step[:, None])
    base = jnp.asarray(np.stack([rep[:, None] < rep[None, :], same]), jnp.float32)

    whole = pl.BlockSpec(memory_space=pltpu.VMEM)
    far = pl.BlockSpec(memory_space=pl.ANY)
    pair_sums = pl.pallas_call(
        functools.partial(pair_kernel, bin_count, seg2),
        out_shape=jax.ShapeDtypeStruct((freqs, 12, LANES), jnp.float32),
        in_specs=[far, whole, far, whole],
        out_specs=whole,
        scratch_shapes=[
            pltpu.VMEM((loop_size, freqs, seg2, channels), jnp.bfloat16),
            pltpu.VMEM((loop_size, 8, LANES), jnp.int32),
            pltpu.VMEM((nch, nch), jnp.bfloat16),
            pltpu.VMEM((groups, LANES, LANES), jnp.float32),
            pltpu.VMEM((groups, LANES, LANES), jnp.float32),
            pltpu.VMEM((nch, 2 * seg2), jnp.bfloat16),
            pltpu.VMEM((groups, 2, 2 * seg2, 2 * LANES), jnp.bfloat16),
            pltpu.SemaphoreType.DMA((freqs // 2, groups - 1)),
            pltpu.SemaphoreType.DMA((freqs // 2, groups - 1)),
            pltpu.SemaphoreType.DMA((groups - 1,)),
            pltpu.SemaphoreType.DMA((groups - 1,)),
            pltpu.SemaphoreType.DMA((3,)),
        ],
        compiler_params=pltpu.CompilerParams(
            vmem_limit_bytes=48 * 2**20, collective_id=0, has_side_effects=True
        ),
        cost_estimate=pl.CostEstimate(
            flops=freqs * nch * nch * seg2 * 2, bytes_accessed=8 * 2**20, transcendentals=0
        ),
    )(x, table, perm, base)

    labels = jnp.arange(bin_count, dtype=jnp.int32)
    col = np.arange(LANES)[:, None] % bin_count
    row = np.arange(bin_count)[None, :]
    none = np.zeros((LANES, bin_count))
    to_bin = np.concatenate(
        [
            np.concatenate([col == row, none], 1),
            np.concatenate([none, col == bin_count - 1 - row], 1),
            np.concatenate([col - 1 == row, none], 1),
        ],
        0,
    ).astype(np.float32)
    binned = jnp.dot(
        pair_sums.reshape(freqs * 4, 3 * LANES),
        jnp.asarray(to_bin),
        precision=lax.Precision.HIGHEST,
    ).reshape(freqs, 4, 2, bin_count)
    sign = jnp.array([1.0, -1.0, 1.0, -1.0], jnp.float32)[None, :, None]
    bins = binned[:, :, 0] + sign * binned[:, :, 1]

    same_owner = bin_owner[:, None] == bin_owner[None, :]
    earlier = labels[None, :] < labels[:, None]
    slot_rank = jnp.sum((same_owner & earlier).astype(jnp.int32), axis=1)
    slot = bin_owner * BCAP + slot_rank
    placement = (
        slot[:, None] == jnp.arange(BCAP * stack_size, dtype=jnp.int32)[None, :]
    ).astype(jnp.float32)
    packed = jnp.einsum("bs,fcb->scf", placement, bins, precision=lax.Precision.HIGHEST)
    devices = stack_size * loop_size
    packed = packed.reshape(devices, BCAP // loop_size, 4, freqs)
    owned = lax.all_to_all(packed, ("stack", "loop"), 0, 0, tiled=True)
    row_total = BCAP // loop_size
    sums = owned.transpose(1, 2, 0, 3).reshape(row_total, 4, devices * freqs)
    linear, weighted = finish(sums[:, 0], sums[:, 1], sums[:, 2], sums[:, 3])
    return (linear.reshape(1, row_total, -1), weighted.reshape(1, row_total, -1))


def solution(mesh):
    in_specs = (P("stack", None, None, "loop"), P("loop"), P("loop"), P())
    out_specs = (P("stack", "loop", None), P("stack", "loop", None))
    return jax.shard_map(
        on_device, mesh=mesh, in_specs=in_specs, out_specs=out_specs, check_vma=False
    )
```

```python
import functools
import math

import jax
import jax.numpy as jnp
import numpy as np
from jax import lax
from jax.experimental import pallas as pl
from jax.experimental.pallas import tpu as pltpu
from jax.sharding import PartitionSpec as P

BCAP = 16
LANES = 128


def lag_matrix(freq_count):
    freq_ids = np.arange(freq_count)
    lag_ids = np.arange(2 * freq_count) - freq_count
    turns = freq_ids[:, None] * lag_ids[None, :] % (2 * freq_count)
    angle = turns * (math.pi / freq_count)
    bin_weight = np.where(freq_ids == 0, 1.0, 2.0)[:, None]
    return np.concatenate(
        [bin_weight * np.cos(angle), -bin_weight * np.sin(angle)], 0
    ).astype(np.float32)


def thirds(value):
    high = value.astype(jnp.bfloat16)
    rest = value - high.astype(jnp.float32)
    middle = rest.astype(jnp.bfloat16)
    low = (rest - middle.astype(jnp.float32)).astype(jnp.bfloat16)
    return high, middle, low


def exact_dot(value, matrix, contract):
    return sum(
        lax.dot_general(
            part, matrix, ((contract[0], contract[1]), ((), ())),
            preferred_element_type=jnp.float32,
        )
        for part in thirds(value)
    )


def pair_kernel(
    bin_count,
    seg2,
    ahead_tiles,
    spectra_ref,
    loc_ref,
    valid_ref,
    perm_hbm,
    base_ref,
    to_bin_ref,
    place_ref,
    lag_hbm,
    linear_ref,
    weighted_ref,
    table_ref,
    part_sums,
    packed,
    shares,
    owned,
    lag_ref,
    series,
    x_ref,
    tables,
    perm_ref,
    keep_ref,
    shift_ref,
    left,
    right,
    send_sem,
    recv_sem,
    table_send,
    table_recv,
    share_send,
    share_recv,
    owned_send,
    owned_recv,
    local_sem,
):
    groups, freqs = x_ref.shape[0], x_ref.shape[1]
    half = seg2 // 2
    reps = LANES // bin_count
    me = lax.axis_index("loop")
    floor = lax.axis_index("stack")
    floors = owned.shape[0]
    tile_rows = owned.shape[1]
    freq_dev = groups * freqs

    def peer(k):
        return lax.rem(me + k, groups)

    def above(k):
        return lax.rem(floor + k, floors)

    first = me * LANES + lax.broadcasted_iota(jnp.int32, (1, LANES), 1)
    table_ref[...] = jnp.zeros_like(table_ref)
    table_ref[0:1] = loc_ref[...] - 2 * first
    table_ref[1:2] = valid_ref[...]

    own = pltpu.make_async_copy(spectra_ref.at[me], x_ref.at[me], local_sem.at[0])
    own.start()
    fetch = pltpu.make_async_copy(perm_hbm, perm_ref, local_sem.at[1])
    fetch.start()
    own_table = pltpu.make_async_copy(table_ref, tables.at[me], local_sem.at[2])
    own_table.start()

    barrier = pltpu.get_barrier_semaphore()
    for k in range(1, groups):
        pl.semaphore_signal(
            barrier, inc=1, device_id={"loop": peer(k)}, device_id_type=pl.DeviceIdType.MESH
        )
    for k in range(1, floors):
        pl.semaphore_signal(
            barrier, inc=1, device_id={"stack": above(k)}, device_id_type=pl.DeviceIdType.MESH
        )
    pl.semaphore_wait(barrier, groups + floors - 2)

    def table_copy(k):
        return pltpu.make_async_remote_copy(
            src_ref=table_ref,
            dst_ref=tables.at[me],
            send_sem=table_send.at[k - 1],
            recv_sem=table_recv.at[k - 1],
            device_id={"loop": peer(k)},
            device_id_type=pl.DeviceIdType.MESH,
        )

    def pair_copy(pair, k):
        return pltpu.make_async_remote_copy(
            src_ref=spectra_ref.at[peer(k), pl.ds(2 * pair, 2)],
            dst_ref=x_ref.at[me, pl.ds(2 * pair, 2)],
            send_sem=send_sem.at[pair, k - 1],
            recv_sem=recv_sem.at[pair, k - 1],
            device_id={"loop": peer(k)},
            device_id_type=pl.DeviceIdType.MESH,
        )

    for k in range(1, groups):
        table_copy(k).start()

    def send_pair(pair, carry):
        for k in range(1, groups):
            pair_copy(pair, k).start()
        return carry

    pairs = freqs // 2
    lax.fori_loop(0, min(ahead_tiles, pairs), send_pair, 0)
    fetch_lag = pltpu.make_async_copy(lag_hbm, lag_ref, local_sem.at[3])

    def fold(block):
        total = block[:bin_count]
        for rep in range(1, reps):
            total = total + block[rep * bin_count : (rep + 1) * bin_count]
        return total

    right[...] = jnp.zeros_like(right)
    part_sums[...] = jnp.zeros_like(part_sums)
    fetch.wait()
    own_table.wait()
    for k in range(1, groups):
        table_copy(k).wait()
    flags = jnp.concatenate([tables[g] for g in range(groups)], 1).astype(jnp.float32)
    valid = flags[1:2].astype(jnp.bfloat16)
    flags = flags.astype(jnp.bfloat16)
    for block in range(groups):
        late = jnp.dot(
            flags,
            perm_ref[:, block * LANES : (block + 1) * LANES],
            preferred_element_type=jnp.float32,
        )[0:1]
        late = jnp.broadcast_to(late, (LANES, LANES))
        early = late.T * (1.0 - late)
        keep_ref[block] = base_ref[0] + base_ref[1] * (1.0 - early)
        shift_ref[block] = base_ref[1] * early
    own.wait()
    fetch_lag.start()

    row_ids = lax.broadcasted_iota(jnp.int32, (bin_count, LANES), 0)
    lane_ids = lax.broadcasted_iota(jnp.int32, (bin_count, LANES), 1)
    ahead = row_ids <= (lane_ids & (bin_count - 1))

    sub_ids = row_ids[:8]

    def turn(part):
        count = bin_count
        while count > 8:
            count //= 2
            part = part[:count] + pltpu.roll(part[count:], LANES - count, 1)
        for step in (4, 2, 1):
            part = jnp.where((sub_ids & step) != 0, pltpu.roll(part, LANES - step, 1), part)
        return part

    def freq_pair(pair, carry):
        @pl.when(pair + ahead_tiles < pairs)
        def _():
            send_pair(pair + ahead_tiles, 0)

        for k in range(1, groups):
            pair_copy(pair, k).wait_recv()
        rows = jnp.concatenate(
            [x_ref[g, pl.ds(2 * pair, 2)].reshape(2 * seg2, LANES) for g in range(groups)], 1
        )
        rows = rows * valid
        for block in range(groups):
            cols = jnp.dot(
                rows,
                perm_ref[:, block * LANES : (block + 1) * LANES],
                preferred_element_type=jnp.float32,
            )
            left[block * LANES : (block + 1) * LANES] = cols.T.astype(jnp.bfloat16)
            for which in range(2):
                at = which * seg2
                re, im = cols[at : at + half], cols[at + half : at + seg2]
                right[block, which, at : at + seg2, :LANES] = cols[at : at + seg2].astype(
                    jnp.bfloat16
                )
                right[block, which, at : at + seg2, LANES:] = jnp.concatenate(
                    [-im, re], 0
                ).astype(jnp.bfloat16)

        def one_freq(which, carry):
            def products(row_block, weights):
                lhs = left[pl.ds(pl.multiple_of(row_block * LANES, LANES), LANES)]
                both = jnp.dot(lhs, weights, preferred_element_type=jnp.float32)
                re, im = both[:, :LANES], both[:, LANES:]
                scale = lax.rsqrt(jnp.maximum(re * re + im * im, 1.0))
                return re, im, re * scale, im * scale

            zero = jnp.zeros((bin_count, LANES), jnp.float32)
            sums, moved = (zero,) * 4, (zero,) * 4
            for block in range(groups):
                weights = right[block, which]

                def add(row_block, sums):
                    parts = products(row_block, weights)
                    return tuple(s + fold(p) for s, p in zip(sums, parts))

                if groups <= 8:
                    for row_block in range(block):
                        sums = add(row_block, sums)
                else:
                    sums = lax.fori_loop(0, block, add, sums)
                parts = products(block, weights)
                keep, shift = keep_ref[block], shift_ref[block]
                sums = tuple(s + fold(p * keep) for s, p in zip(sums, parts))
                moved = tuple(s + fold(p * shift) for s, p in zip(moved, parts))
            spot = (floor * freq_dev + me * freqs + 2 * pair + which) % LANES
            for c in range(4):
                both = (
                    jnp.where(ahead, sums[c], 0.0),
                    jnp.where(ahead, 0.0, sums[c]),
                    moved[c],
                )
                for n, part in enumerate(both):
                    part_sums[3 * c + n, pl.ds(spot, 1)] = jnp.sum(
                        turn(part), axis=0, keepdims=True
                    )
            return carry

        return lax.fori_loop(0, 2, one_freq, carry)

    lax.fori_loop(0, freqs // 2, freq_pair, 0)

    def sent(pair, carry):
        for k in range(1, groups):
            pair_copy(pair, k).wait_send()
        return carry

    rows = jnp.concatenate([part_sums[n] for n in range(12)], 1)
    bins = exact_dot(rows, to_bin_ref[...], ((1,), (0,)))
    packed[...] = sum(
        lax.dot_general(
            place_ref[...], part, (((1,), (1,)), ((), ())), preferred_element_type=jnp.float32
        )
        for part in thirds(bins)
    ).reshape(packed.shape)

    def share_copy(k):
        return pltpu.make_async_remote_copy(
            src_ref=packed.at[peer(k)],
            dst_ref=shares.at[me],
            send_sem=share_send.at[k - 1],
            recv_sem=share_recv.at[k - 1],
            device_id={"loop": peer(k)},
            device_id_type=pl.DeviceIdType.MESH,
        )

    for k in range(1, groups):
        share_copy(k).start()
    shares[me] = packed[me]
    lax.fori_loop(0, pairs, sent, 0)
    for k in range(1, groups):
        share_copy(k).wait()
    total = shares[0]
    for g in range(1, groups):
        total = total + shares[g]
    packed[0] = total

    def owned_copy(k):
        rows = pl.ds(pl.multiple_of(above(k) * tile_rows, tile_rows), tile_rows)
        return pltpu.make_async_remote_copy(
            src_ref=packed.at[0, rows],
            dst_ref=owned.at[floor],
            send_sem=owned_send.at[k - 1],
            recv_sem=owned_recv.at[k - 1],
            device_id={"stack": above(k)},
            device_id_type=pl.DeviceIdType.MESH,
        )

    for k in range(1, floors):
        owned_copy(k).start()
    owned[floor] = packed[0, pl.ds(pl.multiple_of(floor * tile_rows, tile_rows), tile_rows)]
    fetch_lag.wait()
    for k in range(1, floors):
        owned_copy(k).wait()

    tiles = []
    per_tile = max(LANES // freq_dev, 1)
    for start in range(0, floors, per_tile):
        tile = owned[start]
        for more in range(start + 1, start + per_tile):
            tile = tile + owned[more]
        tiles.append(tile)
    spectrum = jnp.concatenate(tiles, 1)
    freq_count = spectrum.shape[1]
    slots = linear_ref.shape[0]
    series[...] = jnp.zeros_like(series)
    for k in range(slots):
        re, im, phase_re, phase_im = (spectrum[4 * k + c : 4 * k + c + 1] for c in range(4))
        coherence = phase_re * phase_re + phase_im * phase_im
        series[k : k + 1, :freq_count] = re
        series[k : k + 1, freq_count:] = im
        series[slots + k : slots + k + 1, :freq_count] = re * coherence
        series[slots + k : slots + k + 1, freq_count:] = im * coherence
    parts = thirds(series[...])
    corr = sum(
        jnp.dot(part, lag_ref[n], preferred_element_type=jnp.float32)
        for n in range(2)
        for part in parts
    )
    power = jnp.mean(corr * corr, axis=1, keepdims=True)
    corr = corr / jnp.sqrt(power + 1e-06)
    linear_ref[...] = corr[:slots]
    weighted_ref[...] = corr[slots : 2 * slots]


def on_device(spectra, channel_loc, channel_valid, bin_owner):
    loop_size = lax.axis_size("loop")
    stack_size = lax.axis_size("stack")
    freq_dev, _, seg, channels = spectra.shape
    bin_count = bin_owner.shape[0]
    groups = loop_size
    nch = groups * channels
    hop = nch // bin_count
    freqs = freq_dev // loop_size
    seg2 = 2 * seg
    reps = LANES // bin_count

    x = spectra.reshape(loop_size, freqs, seg2, channels)
    chan = np.arange(nch)
    place = (chan % hop) * bin_count + chan // hop
    perm = jnp.asarray(place[:, None] == chan[None, :], jnp.bfloat16)
    lane = np.arange(LANES)
    rep, step = lane // bin_count, lane % bin_count
    same = (rep[:, None] == rep[None, :]) & (step[None, :] > step[:, None])
    base = jnp.asarray(np.stack([rep[:, None] < rep[None, :], same]), jnp.float32)

    col = lane[:, None] % bin_count
    row = np.arange(bin_count)[None, :]
    to_bin = np.zeros((4, 3, LANES, 4, bin_count))
    for c in range(4):
        to_bin[c, 0, :, c] = col == row
        to_bin[c, 1, :, c] = (col == bin_count - 1 - row) * (-1.0 if c % 2 else 1.0)
        to_bin[c, 2, :, c] = col - 1 == row
    to_bin = jnp.asarray(to_bin.reshape(12 * LANES, 4 * bin_count), jnp.bfloat16)

    labels = jnp.arange(bin_count, dtype=jnp.int32)
    same_owner = bin_owner[:, None] == bin_owner[None, :]
    earlier = labels[None, :] < labels[:, None]
    slot_rank = jnp.sum((same_owner & earlier).astype(jnp.int32), axis=1)
    slot = bin_owner * BCAP + slot_rank
    slots = BCAP // loop_size
    tile_rows = max(4 * slots, 8)
    line = np.arange(loop_size * stack_size * tile_rows)
    owner = line // tile_rows % stack_size
    number = line // (tile_rows * stack_size) * slots + line % tile_rows // 4
    line_slot = np.where(line % tile_rows < 4 * slots, owner * BCAP + number, -1)
    column = np.arange(4 * bin_count)
    part_match = (line % 4)[:, None] == (column // bin_count)[None, :]
    place = (
        (jnp.tile(slot, 4)[None, :] == jnp.asarray(line_slot, jnp.int32)[:, None]) & part_match
    ).astype(jnp.bfloat16)

    freq_count = freq_dev * stack_size
    matrix = lag_matrix(freq_count)
    high = matrix.astype(jnp.bfloat16)
    low = (matrix - high.astype(np.float32)).astype(jnp.bfloat16)
    lags = jnp.asarray(np.stack([high, low]))

    whole = pl.BlockSpec(memory_space=pltpu.VMEM)
    far = pl.BlockSpec(memory_space=pl.ANY)
    out = jax.ShapeDtypeStruct((slots, 2 * freq_count), jnp.float32)
    linear, weighted = pl.pallas_call(
        functools.partial(pair_kernel, bin_count, seg2, 3),
        out_shape=(out, out),
        in_specs=[far, whole, whole, far, whole, whole, whole, far],
        out_specs=(whole, whole),
        scratch_shapes=[
            pltpu.VMEM((8, LANES), jnp.int32),
            pltpu.VMEM((12, LANES, LANES), jnp.float32),
            pltpu.VMEM((loop_size, stack_size * tile_rows, LANES), jnp.float32),
            pltpu.VMEM((loop_size, stack_size * tile_rows, LANES), jnp.float32),
            pltpu.VMEM((stack_size, tile_rows, LANES), jnp.float32),
            pltpu.VMEM(lags.shape, jnp.bfloat16),
            pltpu.VMEM((8, 2 * freq_count), jnp.float32),
            pltpu.VMEM((loop_size, freqs, seg2, channels), jnp.bfloat16),
            pltpu.VMEM((loop_size, 8, LANES), jnp.int32),
            pltpu.VMEM((nch, nch), jnp.bfloat16),
            pltpu.VMEM((groups, LANES, LANES), jnp.float32),
            pltpu.VMEM((groups, LANES, LANES), jnp.float32),
            pltpu.VMEM((nch, 2 * seg2), jnp.bfloat16),
            pltpu.VMEM((groups, 2, 2 * seg2, 2 * LANES), jnp.bfloat16),
            pltpu.SemaphoreType.DMA((freqs // 2, groups - 1)),
            pltpu.SemaphoreType.DMA((freqs // 2, groups - 1)),
            pltpu.SemaphoreType.DMA((groups - 1,)),
            pltpu.SemaphoreType.DMA((groups - 1,)),
            pltpu.SemaphoreType.DMA((groups - 1,)),
            pltpu.SemaphoreType.DMA((groups - 1,)),
            pltpu.SemaphoreType.DMA((stack_size - 1,)),
            pltpu.SemaphoreType.DMA((stack_size - 1,)),
            pltpu.SemaphoreType.DMA((4,)),
        ],
        compiler_params=pltpu.CompilerParams(
            vmem_limit_bytes=60 * 2**20, collective_id=0, has_side_effects=True
        ),
        cost_estimate=pl.CostEstimate(
            flops=freqs * nch * nch * seg2 * 2, bytes_accessed=8 * 2**20, transcendentals=0
        ),
    )(
        x,
        channel_loc.reshape(1, channels),
        channel_valid.reshape(1, channels),
        perm,
        base,
        to_bin,
        place,
        lags,
    )
    return linear[None], weighted[None]


def solution(mesh):
    in_specs = (P("stack", None, None, "loop"), P("loop"), P("loop"), P())
    out_specs = (P("stack", "loop", None), P("stack", "loop", None))
    return jax.shard_map(
        on_device, mesh=mesh, in_specs=in_specs, out_specs=out_specs, check_vma=False
    )
```
